32 devices in a mesh: region: 16 (over z, y, x), sub: 2 (over core).
Axes of the slice: x: 2, y: 2, z: 4, core: 2. Of those that a mesh axis runs over, the one named last changes fastest.
Arguments:
- probes: float32 [32768, 128], P(('region', 'sub')), may hold values from -6 to 6
- neighbours: int32 [32768, 8], P(('region', 'sub')), may hold values from 0 to 1535, as said below
- lengths: int32 [32768, 8], P(('region', 'sub')), may hold values from 0 to 999, as said below
- iid_precision: float32 [32768], P(('region', 'sub')), may hold values from 0.1 to 2
- send_rows: int32 [64, 256], P(('region', 'sub')), may hold values from 0 to 1023, as said below
Outputs:
- solution: float32 [32768, 128], P(('region', 'sub'))
- trace_terms: float32 [128], replicated
The draws below stay inside these ranges and needn't reach their ends.
Inputs may be any that keep to these rules, and one draw needn't show every extreme that they name: `neighbours`: slots 0 to 5 name rows of the same device; slot 6 names 1024 + b for the b-th row received from device d - 1 or the block itself, slot 7 names 1280 + b for the b-th row received from device d + 1 or the block itself. The weighted links are symmetric across the whole grid, and the first and last devices have no links across their outer side. `lengths`: A slot that names its own block has length 0. `send_rows`: the entries of each row are distinct.
All inputs are finite; a program needn't handle non-finite values.
Results may differ from the reference program's by a relative error of at most 0.0003.
Values sent between devices are 32-bit elements; how exact they have to be, the bound alone decides.
A program may use at most 64 MiB of HBM per device.

```python
import math
import jax
import jax.numpy as jnp
from jax import lax

ROWS = 1024
PROBES = 128
ITERS = 3
LOCAL_PAIRS = 3
GROUP = 8
SLOTS = 8
BOUND = 256
CELLS = 32768


def build_graph(key):
    ndevices = CELLS // ROWS
    pair_keys = jax.random.split(jax.random.fold_in(key, 1), ndevices * LOCAL_PAIRS)
    perms = jax.vmap(lambda k: jax.random.permutation(k, ROWS))(pair_keys).astype(jnp.int32)
    perms = perms.reshape(ndevices, LOCAL_PAIRS, ROWS)
    ngroups = ndevices * (ROWS // GROUP)
    group_keys = jax.random.split(jax.random.fold_in(key, 5), ngroups)
    inside = jax.vmap(lambda k: jax.random.permutation(k, GROUP))(group_keys).astype(jnp.int32)
    inside = inside.reshape(ndevices, ROWS // GROUP, GROUP)
    base = (jnp.arange(ROWS // GROUP, dtype=jnp.int32) * GROUP)[None, :, None]
    inside = (inside + base).reshape(ndevices, ROWS)
    perms = jnp.concatenate([inside[:, None], perms[:, 1:]], axis=1)
    inverse = jnp.argsort(perms, axis=-1, stable=True).astype(jnp.int32)
    rows_local = jnp.arange(ROWS, dtype=jnp.int32)
    not_self = (perms != rows_local[None, None, :]).astype(jnp.int32)
    forward_len = jax.random.randint(jax.random.fold_in(key, 2), (ndevices, LOCAL_PAIRS, ROWS), 1, 1000).astype(jnp.int32)
    forward_len = forward_len * not_self
    back_len = jnp.take_along_axis(forward_len, inverse, axis=-1)
    pick_keys = jax.random.split(jax.random.fold_in(key, 3), ndevices * 2)
    picks = jax.vmap(lambda k: jax.random.permutation(k, ROWS)[:BOUND])(pick_keys).astype(jnp.int32)
    picks = picks.reshape(ndevices, 2, BOUND)
    cross = jax.random.randint(jax.random.fold_in(key, 4), (ndevices, BOUND), 1, 1000).astype(jnp.int32)
    cross = cross * (jnp.arange(ndevices) < ndevices - 1).astype(jnp.int32)[:, None]
    left_len = jnp.concatenate([jnp.zeros((1, BOUND), jnp.int32), cross[:-1]], axis=0)

    def cross_slot(chosen, amount, offset):
        target = rows_local.at[chosen].set(offset + jnp.arange(BOUND, dtype=jnp.int32))
        length = jnp.zeros((ROWS,), jnp.int32).at[chosen].set(amount)
        return (target, length)
    left_target, left_length = jax.vmap(lambda c, a: cross_slot(c, a, ROWS))(picks[:, 0], left_len)
    right_target, right_length = jax.vmap(lambda c, a: cross_slot(c, a, ROWS + BOUND))(picks[:, 1], cross)
    local_target = jnp.stack([perms, inverse], axis=2).reshape(ndevices, 2 * LOCAL_PAIRS, ROWS)
    local_length = jnp.stack([forward_len, back_len], axis=2).reshape(ndevices, 2 * LOCAL_PAIRS, ROWS)
    targets = jnp.concatenate([local_target, left_target[:, None], right_target[:, None]], axis=1)
    amounts = jnp.concatenate([local_length, left_length[:, None], right_length[:, None]], axis=1)
    targets = jnp.transpose(targets, (0, 2, 1)).reshape(CELLS, SLOTS)
    amounts = jnp.transpose(amounts, (0, 2, 1)).reshape(CELLS, SLOTS)
    return (targets, amounts, picks.reshape(ndevices * 2, BOUND))


def draw_neighbours(key, part):
    return build_graph(jax.random.fold_in(key, 7))[0]


def draw_lengths(key, part):
    return build_graph(jax.random.fold_in(key, 7))[1]


def draw_send_rows(key, part):
    return build_graph(jax.random.fold_in(key, 7))[2]


def levels(key, dims, shards, least, high):
    gain = 1.0
    for position, parts in shards:
        steps = jax.random.uniform(jax.random.fold_in(jax.random.fold_in(key, 6), position), (parts,), jnp.float32, least / len(shards), high / len(shards))
        gain = gain * jnp.repeat(jnp.exp(steps), dims[position] // parts).reshape((-1,) + (1,) * (len(dims) - 1 - position))
    return gain


def gaussian(stream_key, shape, deviation, reach, cuts=(), held_as=jnp.bfloat16):
    loudness = levels(stream_key, shape, cuts, -0.22, 0.18) if cuts else 1.0
    values = jax.random.normal(stream_key, shape, jnp.float32) * deviation * loudness
    return jnp.minimum(jnp.maximum(values, -reach), reach).astype(held_as)


def setup_inputs(seed: int = 0) -> dict:
    key_list = jax.random.split(jax.random.key(seed), 6)
    probes = gaussian(key_list[0], (CELLS, PROBES), 1.0, 6.0, ((0, 32),), jnp.float32)
    neighbours = draw_neighbours(jax.random.fold_in(key_list[5], 71), 0)
    lengths = draw_lengths(jax.random.fold_in(key_list[5], 71), 0)
    iid_precision = jnp.clip(jnp.exp(math.log(2.0) - 2.9957323 * jax.random.uniform(key_list[3], (CELLS,), jnp.float32) ** levels(key_list[3], (CELLS,), ((0, 32),), -0.2, 0.2)), 0.1, 2.0)
    send_rows = draw_send_rows(jax.random.fold_in(key_list[5], 71), 0)
    return dict(probes=probes, neighbours=neighbours, lengths=lengths, iid_precision=iid_precision, send_rows=send_rows)


metres_unit = 1000.0

def apply_rows(own, extended, neighbours, weights, center):
    total = center[:, None] * own
    for slot in range(neighbours.shape[1]):
        total = total - weights[:, slot, None] * extended[neighbours[:, slot]]
    return total

def block_inverses(neighbours, weights, center):
    count = neighbours.shape[0]
    index = jnp.arange(count, dtype=jnp.int32)
    columns = (index // GROUP * GROUP)[:, None] + jnp.arange(GROUP, dtype=jnp.int32)[None, :]
    hits = (neighbours[:, :, None] == columns[:, None, :]).astype(jnp.float32)
    offdiag = -jnp.sum(weights[:, :, None] * hits, axis=1)
    ondiag = center[:, None] * (columns == index[:, None]).astype(jnp.float32)
    blocks = (offdiag + ondiag).reshape(count // GROUP, GROUP, GROUP)
    factor = jnp.linalg.cholesky(blocks)
    identity = jnp.broadcast_to(jnp.eye(GROUP, dtype=jnp.float32), blocks.shape)
    lower = lax.linalg.triangular_solve(factor, identity, left_side=True, lower=True)
    return lax.linalg.triangular_solve(factor, lower, left_side=True, lower=True, transpose_a=True)

def precondition(inverse, residual):
    grouped = residual.reshape(inverse.shape[0], GROUP, residual.shape[1])
    return jnp.einsum('gij,gjp->gip', inverse, grouped, precision=lax.Precision.HIGHEST).reshape(residual.shape)

def extend(field, sends):
    toward_next = jax.vmap(lambda rows, picks: rows[picks[1]])(field, sends)
    toward_prev = jax.vmap(lambda rows, picks: rows[picks[0]])(field, sends)
    empty = jnp.zeros_like(toward_next[:1])
    from_left = jnp.concatenate([empty, toward_next[:-1]], axis=0)
    from_right = jnp.concatenate([toward_prev[1:], empty], axis=0)
    return jnp.concatenate([field, from_left, from_right], axis=1)

def reference(probes, neighbours, lengths, iid_precision, send_rows):
    ndevices = CELLS // ROWS
    start = probes.reshape(ndevices, ROWS, PROBES)
    adjacency = neighbours.reshape(ndevices, ROWS, SLOTS)
    weights = lengths.reshape(ndevices, ROWS, SLOTS).astype(jnp.float32) / metres_unit
    links = jnp.sum(weights, axis=2)
    center = links + iid_precision.reshape(ndevices, ROWS)
    sends = send_rows.reshape(ndevices, 2, BOUND)
    inverse = jax.vmap(block_inverses)(adjacency, weights, center)

    def operate(field, diagonal):
        return jax.vmap(apply_rows)(field, extend(field, sends), adjacency, weights, diagonal)

    def inner(first, second):
        return jnp.sum(first * second, axis=(0, 1))
    laplace = operate(start, links)
    solution = jnp.zeros_like(start)
    residual = start
    precond = jax.vmap(precondition)(inverse, residual)
    direction = precond
    gamma = inner(residual, precond)
    for step in range(ITERS):
        image = operate(direction, center)
        alpha = gamma / inner(direction, image)
        solution = solution + alpha * direction
        residual = residual - alpha * image
        precond = jax.vmap(precondition)(inverse, residual)
        gamma_new = inner(residual, precond)
        direction = precond + gamma_new / gamma * direction
        gamma = gamma_new
    trace_terms = inner(solution, laplace) / CELLS
    return (solution.reshape(CELLS, PROBES), trace_terms)
```

```python
import functools

import jax
import jax.numpy as jnp
from jax import lax
from jax.experimental import pallas as pl
from jax.experimental.pallas import tpu as pltpu
from jax.sharding import PartitionSpec as P

GROUP = 8
STEPS = 3
UNIT = 1000.0
BLOCK = 256
LANES = 128
STATS = 16
TINY = 2e-7
F32 = jnp.float32
BF16 = jnp.bfloat16
MESH = pl.DeviceIdType.MESH


def dot(a, b):
    return jnp.dot(a, b, preferred_element_type=F32)


def split(value):
    high = value.astype(BF16)
    return high, (value - high.astype(F32)).astype(BF16)


def halves(value):
    return jnp.concatenate(split(value), axis=1)


def folded(wide):
    half = wide.shape[1] // 2
    return wide[:, :half] + wide[:, half:]


def block_inverse(block):
    lane = lax.broadcasted_iota(jnp.int32, block.shape, 1)
    sub = lax.broadcasted_iota(jnp.int32, block.shape, 0)
    place = lane % GROUP
    for p in range(GROUP):
        col = jnp.take_along_axis(block, lane - place + p, axis=1)
        inv = 1.0 / col[p : p + 1, :]
        row = block[p : p + 1, :] * inv
        rest = block - col * row
        rest = jnp.where(place == p, -col * inv, rest)
        at_row = jnp.where(place[:1] == p, inv, row)
        block = jnp.where(sub == p, at_row, rest)
    return block


def column_sum(value):
    rows, width = value.shape
    return jnp.sum(value.reshape(rows // 8, 8, width).sum(axis=0), axis=0, keepdims=True)


def kernel(
    region, inner,
    nbr_ref, len_ref, iid_ref, send_ref, b_ref,
    x_ref, trace_ref,
    ahi, alo, chi, clo, scat, bdhi, bdlo, off, wide, loc, w, a,
    ysend, yrecv, stats, gathered,
    halo_send, halo_recv, stat_send, stat_recv,
):
    rows, probes = b_ref.shape
    bound = send_ref.shape[1]
    n = region * inner
    me = lax.axis_index("region") * inner + lax.axis_index("sub")

    def device(k):
        return (k // inner, k % inner)

    barrier = pltpu.get_barrier_semaphore()

    def greet(k, carry):
        other = lax.rem(me + k, n)
        pl.semaphore_signal(barrier, inc=1, device_id=device(other), device_id_type=MESH)
        return carry

    lax.fori_loop(1, n, greet, 0)

    def halo(step, side):
        return pltpu.make_async_remote_copy(
            src_ref=ysend.at[step, side],
            dst_ref=yrecv.at[step, side],
            send_sem=halo_send.at[step, side],
            recv_sem=halo_recv.at[step, side],
            device_id=device(lax.rem(me + (1 if side == 0 else n - 1), n)),
            device_id_type=MESH,
        )

    has_next, has_prev = me < n - 1, me > 0

    @pl.when(jnp.logical_not(has_prev))
    def _():
        for step in range(STEPS):
            yrecv[step, 0] = jnp.zeros((bound, probes), F32)

    @pl.when(jnp.logical_not(has_next))
    def _():
        for step in range(STEPS):
            yrecv[step, 1] = jnp.zeros((bound, probes), F32)

    lengths = len_ref[...]
    neighbours = nbr_ref[...]
    weights = lengths.astype(F32) / UNIT
    center = jnp.sum(weights, axis=0, keepdims=True) + iid_ref[...]
    lane = lax.broadcasted_iota(jnp.int32, neighbours.shape, 1)
    sub = lax.broadcasted_iota(jnp.int32, neighbours.shape, 0)
    column = lane - lane % GROUP + sub
    blocks = jnp.where(column == lane, center, 0.0)
    for slot in range(neighbours.shape[0]):
        hit = neighbours[slot : slot + 1] == column
        blocks = blocks - jnp.where(hit, weights[slot : slot + 1], 0.0)
    inside = neighbours // GROUP == lane // GROUP
    off[...] = jnp.where(inside, 0, lengths).astype(F32)
    inverse = jnp.concatenate(
        [block_inverse(blocks[:, s : s + LANES]) for s in range(0, rows, LANES)], axis=1
    )
    across = lax.broadcasted_iota(jnp.int32, (BLOCK, BLOCK), 1) // GROUP
    down = lax.broadcasted_iota(jnp.int32, (BLOCK, BLOCK), 0) // GROUP
    for s in range(0, rows, BLOCK):
        tiled = jnp.concatenate([inverse[:, s : s + BLOCK]] * (BLOCK // GROUP), axis=0)
        bdhi[s : s + BLOCK], bdlo[s : s + BLOCK] = split(jnp.where(across == down, tiled, 0.0))

    def precondition(value_ref, out_ref):
        for s in range(0, rows, BLOCK):
            at = slice(s, s + BLOCK)
            part = halves(value_ref[at])
            out = folded(dot(bdhi[at], part) + dot(bdlo[at], part))
            out_ref[at] = out
            wide[at] = halves(out)

    for side in range(2):
        slot = 7 - side
        high, low = split(len_ref[slot : slot + 1].astype(F32))
        high, low = high.astype(F32), low.astype(F32)
        first = rows + (bound if side == 0 else 0)
        named = lax.broadcasted_iota(jnp.int32, (bound, rows), 0) + first
        hit = nbr_ref[slot : slot + 1] == named
        at = slice(side * bound, (side + 1) * bound)
        chi[at] = jnp.where(hit, high, 0.0).astype(BF16)
        clo[at] = jnp.where(hit, low, 0.0).astype(BF16)

    def send(step):
        for side in range(2):
            at = slice(side * bound, (side + 1) * bound)
            ysend[step, side] = folded(dot(chi[at], wide[...]) + dot(clo[at], wide[...]))

            @pl.when(has_next if side == 0 else has_prev)
            def _():
                halo(step, side).start()

    def build():
        for side in range(2):
            own = lax.broadcasted_iota(jnp.int32, (rows, bound), 0)
            hit = own == send_ref[side : side + 1]
            scat[:, side * bound : (side + 1) * bound] = jnp.where(hit, 1.0, 0.0).astype(BF16)

        def body(i, carry):
            start = pl.multiple_of(i * 16, 16)
            for s in range(0, rows, BLOCK):
                at = slice(s, s + BLOCK)
                named = lax.broadcasted_iota(jnp.int32, (16, BLOCK), 0) + start
                total = jnp.zeros((16, BLOCK), F32)
                for slot in range(6):
                    hit = nbr_ref[slot : slot + 1, at] == named
                    total = total + jnp.where(hit, off[slot : slot + 1, at], 0.0)
                high, low = split(total)
                ahi[pl.ds(start, 16), at] = high
                alo[pl.ds(start, 16), at] = low
            return carry

        lax.fori_loop(0, rows // 16, body, 0)

    def local():
        def body(i, carry):
            at = pl.ds(pl.multiple_of(i * BLOCK, BLOCK), BLOCK)
            loc[at] = folded(dot(ahi[at], wide[...]) + dot(alo[at], wide[...]))
            return carry

        lax.fori_loop(0, rows // BLOCK, body, 0)

    def receive(step):
        @pl.when(has_prev)
        def _():
            halo(step, 0).wait_recv()

        @pl.when(has_next)
        def _():
            halo(step, 1).wait_recv()

        part = jnp.concatenate([halves(yrecv[step, side]) for side in range(2)], axis=0)
        for s in range(0, rows, BLOCK):
            at = slice(s, s + BLOCK)
            a[step, at] = (folded(dot(scat[at], part)) + loc[at]) * (1.0 / UNIT)

    pl.semaphore_wait(barrier, n - 1)
    precondition(b_ref, w.at[0])
    for step in range(STEPS):
        send(step)
        if step == 0:
            build()
        local()
        receive(step)
        if step + 1 < STEPS:
            precondition(a.at[step], w.at[step + 1])

    b = b_ref[...]
    iid = jnp.broadcast_to(iid_ref[...], (8, rows))

    def scaled(value):
        return jnp.dot(iid, value, precision=lax.Precision.HIGHEST, preferred_element_type=F32)[:1]

    ba = [column_sum(b * a[k]) for k in range(3)]
    bw = [b * w[k] for k in range(3)]
    lines = [
        column_sum(bw[0]),
        column_sum(bw[1]),
        column_sum(a[0] * w[1]),
        column_sum(a[1] * w[1]),
        column_sum(a[1] * w[2]),
        column_sum(a[2] * w[2]),
        column_sum(b * b) - ba[0] - scaled(bw[0]),
        ba[0] - ba[1] - scaled(bw[1]),
        ba[1] - ba[2] - scaled(bw[2]),
    ]
    lines = lines + [jnp.zeros_like(lines[0])] * (STATS - len(lines))
    stats[...] = jnp.concatenate(lines, axis=0)

    def tell(k):
        other = lax.rem(me + k, n)
        return pltpu.make_async_remote_copy(
            src_ref=stats,
            dst_ref=gathered.at[k],
            send_sem=stat_send.at[k],
            recv_sem=stat_recv.at[k],
            device_id=device(other),
            device_id_type=MESH,
        )

    def start_tell(k, carry):
        tell(k).start()
        return carry

    def wait_tell(k, carry):
        tell(k).wait_recv()
        return carry

    lax.fori_loop(1, n, start_tell, 0)
    gathered[0] = stats[...]
    lax.fori_loop(1, n, wait_tell, 0)
    sums = jnp.sum(gathered[...], axis=0)
    m = [sums[k : k + 1] for k in range(9)]

    d = [m[k] - m[k + 1] for k in range(5)]

    def inverse_pivot(pivot, diagonal):
        usable = pivot > TINY * diagonal
        return jnp.where(usable, 1.0 / jnp.where(usable, pivot, 1.0), 0.0)

    i0 = inverse_pivot(d[0], d[0])
    l10, l20 = d[1] * i0, d[2] * i0
    i1 = inverse_pivot(d[2] - l10 * d[1], d[2])
    e21 = d[3] - l20 * d[1]
    l21 = e21 * i1
    i2 = inverse_pivot(d[4] - l20 * d[2] - l21 * e21, d[4])
    y0 = m[0]
    y1 = m[1] - l10 * y0
    y2 = m[2] - l20 * y0 - l21 * y1
    c2 = y2 * i2
    c1 = y1 * i1 - l21 * c2
    c0 = y0 * i0 - l10 * c1 - l20 * c2
    x_ref[...] = c0 * w[0] + c1 * w[1] + c2 * w[2]
    trace_ref[...] = (c0 * m[6] + c1 * m[7] + c2 * m[8]) / (n * rows)

    for step in range(STEPS):
        @pl.when(has_next)
        def _():
            halo(step, 0).wait_send()

        @pl.when(has_prev)
        def _():
            halo(step, 1).wait_send()

    def end_tell(k, carry):
        tell(k).wait_send()
        return carry

    lax.fori_loop(1, n, end_tell, 0)


def on_device(region, inner, probes, neighbours, lengths, iid_precision, send_rows):
    rows, width = probes.shape
    bound = send_rows.shape[1]
    n = region * inner
    vmem = pl.BlockSpec(memory_space=pltpu.VMEM)
    x, trace = pl.pallas_call(
        functools.partial(kernel, region, inner),
        out_shape=(
            jax.ShapeDtypeStruct((rows, width), F32),
            jax.ShapeDtypeStruct((1, width), F32),
        ),
        in_specs=[vmem] * 5,
        out_specs=(vmem, vmem),
        scratch_shapes=[
            pltpu.VMEM((rows, rows), BF16),
            pltpu.VMEM((rows, rows), BF16),
            pltpu.VMEM((2 * bound, rows), BF16),
            pltpu.VMEM((2 * bound, rows), BF16),
            pltpu.VMEM((rows, 2 * bound), BF16),
            pltpu.VMEM((rows, BLOCK), BF16),
            pltpu.VMEM((rows, BLOCK), BF16),
            pltpu.VMEM((neighbours.shape[1], rows), F32),
            pltpu.VMEM((rows, 2 * width), BF16),
            pltpu.VMEM((rows, width), F32),
            pltpu.VMEM((STEPS, rows, width), F32),
            pltpu.VMEM((STEPS, rows, width), F32),
            pltpu.VMEM((STEPS, 2, bound, width), F32),
            pltpu.VMEM((STEPS, 2, bound, width), F32),
            pltpu.VMEM((STATS, width), F32),
            pltpu.VMEM((n, STATS, width), F32),
            pltpu.SemaphoreType.DMA((STEPS, 2)),
            pltpu.SemaphoreType.DMA((STEPS, 2)),
            pltpu.SemaphoreType.DMA((n,)),
            pltpu.SemaphoreType.DMA((n,)),
        ],
        compiler_params=pltpu.CompilerParams(
            collective_id=0, has_side_effects=True, vmem_limit_bytes=48 * 2**20
        ),
        name="trace_gradient",
    )(neighbours.T, lengths.T, iid_precision.reshape(1, rows), send_rows, probes)
    return x, trace.reshape(width)


def solution(mesh):
    return jax.shard_map(
        functools.partial(on_device, mesh.shape["region"], mesh.shape["sub"]),
        mesh=mesh,
        in_specs=(
            P(("region", "sub"), None),
            P(("region", "sub"), None),
            P(("region", "sub"), None),
            P(("region", "sub")),
            P(("region", "sub"), None),
        ),
        out_specs=(P(("region", "sub"), None), P()),
        check_vma=False,
    )
```
